512 devices in a mesh: dp: 32 (over x, y), tensor: 16 (over z, core).
Axes of the slice: x: 4, y: 8, z: 8, core: 2. Of those that a mesh axis runs over, the one named last changes fastest.
Arguments:
- activations: bfloat16 [32, 1024, 2048], P('dp', 'tensor'), may hold values from -6 to 6
- out_grad: bfloat16 [32, 1024, 7168], P('dp', None, 'tensor'), may hold values from -0.1875 to 0.1875
- feedback: bfloat16 [32, 2048, 7168], P('dp', None, 'tensor'), may hold values from -3 to 3
- q_prev: float32 [7168, 64], P('tensor'), may hold values from -6 to 6
Outputs:
- new_feedback: bfloat16 [32, 2048, 7168], P('dp', None, 'tensor')
- p_orth: float32 [2048, 64], P('tensor')
- q_new: float32 [7168, 64], P('tensor')
The draws below stay inside these ranges and needn't reach their ends.
All inputs are finite; a program needn't handle non-finite values.
Results may differ from the reference program's by a relative error of at most 0.00045.
Values may be sent and summed in bfloat16 or wider, within the bound.
No kernel may reach another device: no remote copies, remote signals or barrier semaphores. Data moves between devices by JAX's collectives and lax.ppermute only.
A program may use at most 64 MiB of HBM per device.

```python
import jax
import jax.numpy as jnp
from jax import lax

D = 2048
FF = 7168
RANK = 64
TOK = 1024
REPLICAS = 32


def levels(stream_key, dims, cuts, low, largest):
    level = 1.0
    for dim, blocks in cuts:
        heights = jax.random.uniform(jax.random.fold_in(jax.random.fold_in(stream_key, 6), dim), (blocks,), jnp.float32, low / len(cuts), largest / len(cuts))
        level = level * jnp.repeat(jnp.exp(heights), dims[dim] // blocks).reshape((-1,) + (1,) * (len(dims) - 1 - dim))
    return level


def noise(stream_key, shape, spread, limit, pieces=(), held_as=jnp.bfloat16):
    gain = levels(stream_key, shape, pieces, -0.22, 0.18) if pieces else 1.0
    result = jax.random.normal(stream_key, shape, jnp.float32) * spread * gain
    return jnp.minimum(jnp.maximum(result, -limit), limit).astype(held_as)


def setup_inputs(seed: int = 0) -> dict:
    streams_of = jax.random.split(jax.random.key(seed), 5)
    return {
        "activations": noise(streams_of[0], (REPLICAS, TOK, D), 1.0, 6.0, ((0, 32), (1, 16))),
        "out_grad": noise(streams_of[1], (REPLICAS, TOK, FF), 0.03125, 0.1875, ((0, 32), (2, 16))),
        "feedback": noise(streams_of[2], (REPLICAS, D, FF), 0.5, 3.0, ((0, 32), (2, 16))),
        "q_prev": noise(streams_of[3], (FF, RANK), 1.0, 6.0, ((0, 16),), jnp.float32),
    }


def orthonormal(matrix):
    columns = matrix.shape[1]
    order = jnp.arange(columns)

    def sweep(position, current):
        column = current[:, position]
        column = column / jnp.sqrt(jnp.sum(column * column) + 1e-06)
        projected = jnp.dot(column, current, precision=lax.Precision.HIGHEST)
        later = jnp.where(order > position, projected, jnp.zeros_like(projected))
        current = current - column[:, None] * later[None, :]
        return jnp.where((order == position)[None, :], column[:, None], current)
    return lax.fori_loop(0, columns, sweep, matrix)

def reference(activations, out_grad, feedback, q_prev):

    def corrected_of(items):
        inputs, cotangent, stored = items
        grad_part = lax.dot_general(inputs, cotangent, (((0,), (0,)), ((), ())), preferred_element_type=jnp.float32)
        return grad_part + stored.astype(jnp.float32)
    corrected = lax.map(corrected_of, (activations, out_grad, feedback))
    p_sum = jnp.einsum('rdf,fk->dk', corrected, q_prev, precision=lax.Precision.HIGHEST) / REPLICAS
    p_orth = orthonormal(p_sum)
    q_new = jnp.einsum('rdf,dk->fk', corrected, p_orth, precision=lax.Precision.HIGHEST) / REPLICAS
    decompressed = jnp.dot(p_orth, q_new.T, precision=lax.Precision.HIGHEST)
    new_feedback = (corrected - decompressed[None]).astype(jnp.bfloat16)
    return (new_feedback, p_orth, q_new)
```

```python
import jax
import jax.numpy as jnp
from jax import lax
from jax.experimental import pallas as pl
from jax.experimental.pallas import tpu as pltpu
from jax.sharding import Mesh
from jax.sharding import PartitionSpec as P

LANES = 128
SUBLANES = 8
EPS = 1e-06
BF16 = jnp.bfloat16
F32 = jnp.float32


def split3(value):
    high = value.astype(BF16)
    rest = value - high.astype(F32)
    middle = rest.astype(BF16)
    low = (rest - middle.astype(F32)).astype(BF16)
    return high, middle, low


def stacked(value):
    return jnp.concatenate(split3(value), axis=0)


def unstacked(value):
    rows = value.shape[0] // 3
    return (value[2 * rows :] + value[rows : 2 * rows]) + value[:rows]


def exact_dot(value, exact):
    return unstacked(jnp.dot(stacked(value), exact, preferred_element_type=F32))


def exact_dot_t(value, exact):
    return unstacked(
        lax.dot_general(
            stacked(value), exact, (((1,), (1,)), ((), ())), preferred_element_type=F32
        )
    )


def call(kernel, out_shape, *args, grid=None, vmem=32, **kw):
    shapes = jax.tree.map(lambda s: jax.ShapeDtypeStruct(*s), out_shape, is_leaf=lambda s: isinstance(s, tuple) and isinstance(s[0], tuple))
    return pl.pallas_call(
        kernel,
        out_shape=shapes,
        compiler_params=pltpu.CompilerParams(vmem_limit_bytes=vmem * 2**20),
        **({} if grid is None else {"grid": grid}),
        **kw,
    )(*args)


def cotangent_kernel(q_ref, g_ref, out_ref):
    rank = q_ref.shape[0]
    half = rank // 2
    product = exact_dot(q_ref[...], g_ref[...])
    low = lax.broadcasted_iota(jnp.int32, (half, LANES), 1) < LANES // 2
    for tile in range(product.shape[1] // LANES):
        block = product[:, tile * LANES : (tile + 1) * LANES]
        top, bottom = block[:half], block[half:]
        out_ref[2 * tile] = jnp.where(low, top, pltpu.roll(bottom, LANES // 2, 1))
        out_ref[2 * tile + 1] = jnp.where(low, pltpu.roll(top, LANES // 2, 1), bottom)


def feedback_kernel(q_ref, f_ref, out_ref):
    product = exact_dot(q_ref[...], f_ref[...])
    for tile in range(out_ref.shape[0]):
        out_ref[tile] = product[:, tile * LANES : (tile + 1) * LANES]


def left_kernel(y_ref, a_ref, pf_ref, out_ref):
    total = y_ref[0]
    for source in range(1, y_ref.shape[0]):
        total = total + y_ref[source]
    tokens = a_ref.shape[0]
    mine = jnp.concatenate([total[:, :tokens], total[:, tokens:]], axis=0)
    product = exact_dot(mine, a_ref[...])
    for tile in range(out_ref.shape[0]):
        out_ref[tile] = product[:, tile * LANES : (tile + 1) * LANES] + pf_ref[tile]


def pair_kernel(x_ref, out_ref):
    out_ref[...] = x_ref[0] + x_ref[1]


def share_kernel(fold, scale, x_ref, out_ref):
    total = x_ref[0]
    for source in range(1, x_ref.shape[0]):
        total = total + x_ref[source]
    step = fold
    while step < SUBLANES:
        total = total + pltpu.roll(total, step, 0)
        step *= 2
    total = total * scale
    for target in range(out_ref.shape[0]):
        out_ref[target] = total


def orthonormal_kernel(core_ref, mine_ref, other_ref, x_ref):
    tiles, rank, _ = x_ref.shape
    part = tiles // 2
    core = core_ref[0]
    x_ref[pl.ds(core * part, part)] = mine_ref[...]
    x_ref[pl.ds((1 - core) * part, part)] = other_ref[...]
    for first in range(0, rank, SUBLANES):

        def sweep(step, carry, first=first):
            position = first + step
            rows = [x_ref[tile, pl.ds(position, 1), :] for tile in range(tiles)]
            dots = x_ref[0, first:, :] * rows[0]
            square = rows[0] * rows[0]
            for tile in range(1, tiles):
                dots = dots + x_ref[tile, first:, :] * rows[tile]
                square = square + rows[tile] * rows[tile]
            dots = jnp.sum(dots, axis=1, keepdims=True)
            square = jnp.sum(square, axis=1, keepdims=True) + EPS
            order = lax.broadcasted_iota(jnp.int32, dots.shape, 0) + first
            factor = jnp.where(order > position, dots / square, 0.0)
            scale = jnp.where(order == position, 1.0 / jnp.sqrt(square), 1.0)
            for tile in range(tiles):
                x_ref[tile, first:, :] = x_ref[tile, first:, :] * scale - rows[tile] * factor
            return carry

        lax.fori_loop(0, SUBLANES, sweep, 0)


def wide(p_ref):
    return jnp.concatenate([p_ref[tile] for tile in range(p_ref.shape[0])], axis=1)


def right_kernel(p_ref, a_ref, f_ref, g_ref, out_ref):
    p = wide(p_ref)
    tokens = exact_dot_t(p, a_ref[...])
    product = exact_dot_t(p, f_ref[...]) + exact_dot_t(tokens, g_ref[...])
    width = product.shape[1]
    for tile in range(out_ref.shape[0]):
        block = product[:, tile * LANES : min(width, (tile + 1) * LANES)]
        if block.shape[1] < LANES:
            block = jnp.concatenate([block, jnp.zeros((block.shape[0], LANES - block.shape[1]), F32)], axis=1)
        out_ref[tile] = block


def feedback_out_kernel(q_ref, p_ref, g_ref, a_ref, f_ref, fb_ref, qt_ref):
    width = qt_ref.shape[1]
    q_wide = wide(q_ref)[:, :width]
    qt_ref[...] = q_wide
    q1, q2, q3 = split3(q_wide.T)
    p1, p2, p3 = split3(wide(p_ref))
    left = jnp.concatenate([q3, q1, q2, q2, q1, q1], axis=1)
    right = jnp.concatenate([p1, p3, p2, p1, p2, p1], axis=0)
    low_rank = jnp.dot(left, right, preferred_element_type=F32)
    gradient = jnp.dot(g_ref[...], a_ref[...], preferred_element_type=F32)
    corrected = gradient + f_ref[...].astype(F32)
    fb_ref[...] = (corrected - low_rank).astype(BF16)


def body(activations, out_grad, feedback, q_prev):
    xy, xyz, tensor = ("x", "y"), ("x", "y", "z"), ("z", "c")
    a = activations[0]
    gt = out_grad[0].T
    ft = feedback[0].T
    qt = q_prev.T
    width, columns = ft.shape[1], ft.shape[0]
    rank, tokens = qt.shape[0], gt.shape[1]
    replicas = lax.axis_size(xy)
    chips = lax.axis_size(xyz)
    members = lax.axis_size(tensor)
    core = lax.axis_index("c")
    tiles = width // LANES

    a_full = lax.all_gather(a, tensor, axis=0, tiled=True)
    y = call(cotangent_kernel, ((members, rank // 2, LANES), F32), qt, gt)
    y = lax.all_to_all(y, tensor, 0, 0)
    p_feedback = call(feedback_kernel, ((tiles, rank, LANES), F32), qt, ft)
    p = call(left_kernel, ((tiles, rank, LANES), F32), y, a, p_feedback)
    p = lax.all_to_all(p.reshape(2, tiles // 2 * rank, LANES), "c", 0, 0)
    p = call(pair_kernel, ((tiles // 2 * rank, LANES), F32), p)
    rows = tiles // 2 * rank // chips
    groups = tiles // 2 * rank // SUBLANES
    p = lax.all_to_all(p.reshape(chips, rows, LANES), xyz, 0, 0)
    p = call(
        lambda *refs: share_kernel(rows, 1.0 / replicas, *refs),
        ((groups, SUBLANES, LANES), F32),
        p.reshape(groups, SUBLANES, LANES),
    )
    p = lax.all_to_all(p.reshape(chips, rows, LANES), xyz, 0, 0)
    p = p.reshape(tiles // 2, rank, LANES)
    other = lax.ppermute(p, "c", [(0, 1), (1, 0)])
    vmem = pl.BlockSpec(memory_space=pltpu.VMEM)
    p_orth = call(
        orthonormal_kernel,
        ((tiles, rank, LANES), F32),
        core.astype(jnp.int32)[None],
        p,
        other,
        in_specs=[pl.BlockSpec(memory_space=pltpu.SMEM), vmem, vmem],
        out_specs=vmem,
    )
    p_mine = lax.dynamic_index_in_dim(p_orth, lax.axis_index(tensor), 0, keepdims=False).T

    q_tiles = -(-columns // LANES)
    q = call(right_kernel, ((q_tiles, rank, LANES), F32), p_orth, a_full, ft, gt)
    q_rows = q_tiles * rank // replicas
    q_groups = q_tiles * rank // SUBLANES
    q = lax.all_to_all(q.reshape(replicas, q_rows, LANES), xy, 0, 0)
    q = call(
        lambda *refs: share_kernel(q_rows, 1.0 / replicas, *refs),
        ((q_groups, SUBLANES, LANES), F32),
        q.reshape(q_groups, SUBLANES, LANES),
    )
    q = lax.all_to_all(q.reshape(replicas, q_rows, LANES), xy, 0, 0)
    q = q.reshape(q_tiles, rank, LANES)

    block = 2 * LANES
    fbt, q_new = call(
        feedback_out_kernel,
        [((columns, width), BF16), ((rank, columns), F32)],
        q,
        p_orth,
        gt,
        a_full,
        ft,
        grid=(width // block,),
        in_specs=[
            pl.BlockSpec((q_tiles, rank, LANES), lambda i: (0, 0, 0)),
            pl.BlockSpec((block // LANES, rank, LANES), lambda i: (i, 0, 0)),
            pl.BlockSpec((columns, tokens), lambda i: (0, 0)),
            pl.BlockSpec((tokens, block), lambda i: (0, i)),
            pl.BlockSpec((columns, block), lambda i: (0, i)),
        ],
        out_specs=[
            pl.BlockSpec((columns, block), lambda i: (0, i)),
            pl.BlockSpec((rank, columns), lambda i: (0, 0)),
        ],
    )
    return fbt.T[None], p_mine, q_new.T


def solution(mesh):
    sizes = (4, 8, 8, 2)
    fine = Mesh(mesh.devices.reshape(sizes), ("x", "y", "z", "c"))
    dp, tensor = ("x", "y"), ("z", "c")
    in_specs = (
        P(dp, tensor, None),
        P(dp, None, tensor),
        P(dp, None, tensor),
        P(tensor, None),
    )
    out_specs = (P(dp, None, tensor), P(tensor, None), P(tensor, None))
    return jax.shard_map(body, mesh=fine, in_specs=in_specs, out_specs=out_specs, check_vma=False)
```

```python
import jax
import jax.numpy as jnp
from jax import lax
from jax.experimental import pallas as pl
from jax.experimental.pallas import tpu as pltpu
from jax.sharding import Mesh
from jax.sharding import PartitionSpec as P

LANES = 128
SUBLANES = 8
EPS = 1e-06
BF16 = jnp.bfloat16
F32 = jnp.float32


def split3(value):
    high = value.astype(BF16)
    rest = value - high.astype(F32)
    middle = rest.astype(BF16)
    low = (rest - middle.astype(F32)).astype(BF16)
    return high, middle, low


def stacked(value):
    return jnp.concatenate(split3(value), axis=0)


def unstacked(value):
    rows = value.shape[0] // 3
    return (value[2 * rows :] + value[rows : 2 * rows]) + value[:rows]


def exact_dot(value, exact):
    return unstacked(jnp.dot(stacked(value), exact, preferred_element_type=F32))


def exact_dot_t(value, exact):
    return unstacked(
        lax.dot_general(
            stacked(value), exact, (((1,), (1,)), ((), ())), preferred_element_type=F32
        )
    )


def call(kernel, out_shape, *args, grid=None, vmem=12, **kw):
    shapes = jax.tree.map(lambda s: jax.ShapeDtypeStruct(*s), out_shape, is_leaf=lambda s: isinstance(s, tuple) and isinstance(s[0], tuple))
    return pl.pallas_call(
        kernel,
        out_shape=shapes,
        compiler_params=pltpu.CompilerParams(vmem_limit_bytes=vmem * 2**20),
        **({} if grid is None else {"grid": grid}),
        **kw,
    )(*args)


def started(sources, targets, sems):
    copies = [pltpu.make_async_copy(*pair, sems.at[i]) for i, pair in enumerate(zip(sources, targets))]
    for copy in copies:
        copy.start()
    return copies


def fetched(sources, targets, sems):
    for copy in started(sources, targets, sems):
        copy.wait()


def cotangent_kernel(q_hbm, g_hbm, out_ref, q_ref, g_ref, sems):
    fetched((q_hbm, g_hbm), (q_ref, g_ref), sems)
    rank = q_ref.shape[0]
    half = rank // 2
    product = exact_dot(q_ref[...], g_ref[...])
    low = lax.broadcasted_iota(jnp.int32, (half, LANES), 1) < LANES // 2
    for tile in range(product.shape[1] // LANES):
        block = product[:, tile * LANES : (tile + 1) * LANES]
        top, bottom = block[:half], block[half:]
        out_ref[2 * tile] = jnp.where(low, top, pltpu.roll(bottom, LANES // 2, 1))
        out_ref[2 * tile + 1] = jnp.where(low, pltpu.roll(top, LANES // 2, 1), bottom)


def feedback_kernel(q_ref, f_ref, out_ref):
    product = exact_dot(q_ref[...], f_ref[...])
    for tile in range(out_ref.shape[0]):
        out_ref[tile] = product[:, tile * LANES : (tile + 1) * LANES]


def left_kernel(y_ref, a_ref, pf_ref, out_ref):
    total = y_ref[0]
    for source in range(1, y_ref.shape[0]):
        total = total + y_ref[source]
    tokens = a_ref.shape[0]
    mine = jnp.concatenate([total[:, :tokens], total[:, tokens:]], axis=0)
    product = exact_dot(mine, a_ref[...])
    for tile in range(out_ref.shape[0]):
        out_ref[tile] = product[:, tile * LANES : (tile + 1) * LANES] + pf_ref[tile]


def pair_kernel(x_ref, out_ref):
    out_ref[...] = x_ref[0] + x_ref[1]


def share_kernel(scale, x_ref, out_ref):
    total = x_ref[0]
    for source in range(1, x_ref.shape[0]):
        total = total + x_ref[source]
    total = total * scale
    for target in range(out_ref.shape[0]):
        out_ref[target] = total


def share(x, targets, scale):
    return call(lambda *refs: share_kernel(scale, *refs), ((targets,) + x.shape[1:], F32), x)


def tree_sum(values):
    while len(values) > 1:
        values = [sum(values[i : i + 2]) for i in range(0, len(values), 2)]
    return values[0]


def lane_sum(values):
    return jnp.sum(tree_sum(values), axis=1, keepdims=True)


def orthonormal(x_ref):
    tiles, rank, _ = x_ref.shape
    index = lax.broadcasted_iota(jnp.int32, (SUBLANES, 1), 0)
    for first in range(0, rank, SUBLANES):
        group = [x_ref[tile, first : first + SUBLANES, :] for tile in range(tiles)]
        squares = jnp.ones((SUBLANES, 1), F32)
        for position in range(SUBLANES):
            rows = [value[position : position + 1, :] for value in group]
            dots = lane_sum([value * row for value, row in zip(group, rows)])
            square = dots[position : position + 1, :] + EPS
            squares = jnp.where(index == position, square, squares)
            if position + 1 < SUBLANES:
                factor = jnp.where(index > position, dots / square, 0.0)
                group = [value - row * factor for value, row in zip(group, rows)]
        scale = 1.0 / jnp.sqrt(squares)
        group = [value * scale for value in group]
        for tile in range(tiles):
            x_ref[tile, first : first + SUBLANES, :] = group[tile]
        if first + SUBLANES == rank:
            break
        overlaps = [
            lane_sum([value * value[position : position + 1, :] for value in group])
            for position in range(SUBLANES - 1)
        ]
        for later in range(first + SUBLANES, rank, SUBLANES):
            values = [x_ref[tile, later : later + SUBLANES, :] for tile in range(tiles)]
            factors = []
            for position in range(SUBLANES):
                row = first + position
                factor = lane_sum([values[tile] * x_ref[tile, row : row + 1, :] for tile in range(tiles)])
                for before in range(position):
                    factor = factor - factors[before] * overlaps[before][position : position + 1, :]
                factors.append(factor)
            for tile in range(tiles):
                change = tree_sum(
                    [x_ref[tile, first + i : first + i + 1, :] * factors[i] for i in range(SUBLANES)]
                )
                x_ref[tile, later : later + SUBLANES, :] = values[tile] - change


def wide(p_ref):
    return jnp.concatenate([p_ref[tile] for tile in range(p_ref.shape[0])], axis=1)


def pair_dot_t(value, exact):
    rows = value.shape[0]
    high, middle, _ = split3(value)
    product = lax.dot_general(
        jnp.concatenate([high, middle], axis=0),
        exact,
        (((1,), (1,)), ((), ())),
        preferred_element_type=F32,
    )
    return product[rows:] + product[:rows]


def factors_kernel(
    place_ref, mine_hbm, other_hbm, a_hbm, f_hbm, g_hbm,
    p_hbm, p_mine_ref, out_ref,
    p_ref, a_ref, f_ref, g_ref, sems,
):
    tiles = p_ref.shape[0]
    part = tiles // 2
    member, core = place_ref[0], place_ref[1]
    mine, other = p_ref.at[pl.ds(core * part, part)], p_ref.at[pl.ds((1 - core) * part, part)]
    copies = started((mine_hbm, other_hbm, a_hbm, f_hbm, g_hbm), (mine, other, a_ref, f_ref, g_ref), sems)
    copies[0].wait()
    copies[1].wait()
    orthonormal(p_ref)
    written = pltpu.make_async_copy(p_ref, p_hbm, sems.at[0])
    written.start()
    p_mine_ref[...] = p_ref[member]
    p = wide(p_ref)
    for copy in copies[2:]:
        copy.wait()
    product = pair_dot_t(p, f_ref[...])
    product = product + pair_dot_t(pair_dot_t(p, a_ref[...]), g_ref[...])
    width = product.shape[1]
    for tile in range(out_ref.shape[0]):
        block = product[:, tile * LANES : min(width, (tile + 1) * LANES)]
        if block.shape[1] < LANES:
            block = jnp.concatenate([block, jnp.zeros((block.shape[0], LANES - block.shape[1]), F32)], axis=1)
        out_ref[tile] = block
    written.wait()


def corrected_kernel(a_ref, g_ref, f_ref, out_ref):
    product = jnp.dot(g_ref[...], a_ref[...], preferred_element_type=F32)
    out_ref[...] = product + f_ref[...].astype(F32)


def feedback_out_kernel(q_hbm, p_hbm, c_hbm, fb_hbm, qt_ref, q_ref, p_ref, c_ref, fb_ref, sems, c_sems, fb_sems):
    steps = c_sems.shape[0]
    step = c_ref.shape[1] // steps
    copies = started((q_hbm, p_hbm), (q_ref, p_ref), sems)
    slices = [pl.ds(i * step, step) for i in range(steps)]
    reads = started([c_hbm.at[:, at] for at in slices], [c_ref.at[:, at] for at in slices], c_sems)
    writes = [
        pltpu.make_async_copy(fb_ref.at[:, at], fb_hbm.at[:, at], fb_sems.at[i]) for i, at in enumerate(slices)
    ]
    copies[0].wait()
    q_wide = wide(q_ref)[:, : qt_ref.shape[1]]
    qt_ref[...] = q_wide
    q1, q2, _ = split3(q_wide.T)
    left = jnp.concatenate([q2, q2, q1, q1], axis=1)
    copies[1].wait()
    for i, at in enumerate(slices):
        p1, p2, _ = split3(jnp.concatenate([p_ref[t] for t in range(i * step // LANES, (i + 1) * step // LANES)], axis=1))
        right = jnp.concatenate([p2, p1, p2, p1], axis=0)
        low_rank = jnp.dot(left, right, preferred_element_type=F32)
        reads[i].wait()
        fb_ref[:, at] = (c_ref[:, at] - low_rank).astype(BF16)
        writes[i].start()
    for write in writes:
        write.wait()


def body(activations, out_grad, feedback, q_prev):
    xy, tensor = ("x", "y"), ("z", "c")
    a = activations[0]
    gt = out_grad[0].T
    ft = feedback[0].T
    qt = q_prev.T
    width, columns = ft.shape[1], ft.shape[0]
    rank, tokens = qt.shape[0], gt.shape[1]
    replicas = lax.axis_size(xy)
    members = lax.axis_size(tensor)
    tiles = width // LANES

    swap = [(0, 1), (1, 0)]
    vmem = pl.BlockSpec(memory_space=pltpu.VMEM)
    smem = pl.BlockSpec(memory_space=pltpu.SMEM)
    anywhere = pl.BlockSpec(memory_space=pl.ANY)

    y = call(
        cotangent_kernel,
        ((members, rank // 2, LANES), F32),
        qt,
        gt,
        in_specs=[anywhere, anywhere],
        out_specs=vmem,
        scratch_shapes=[pltpu.VMEM(qt.shape, F32), pltpu.VMEM(gt.shape, BF16), pltpu.SemaphoreType.DMA((2,))],
        vmem=57,
    )
    y = lax.all_to_all(y, tensor, 0, 0)
    a_full = lax.all_gather(a, tensor, axis=0, tiled=True)
    layers = lax.axis_size("z")

    p_feedback = call(feedback_kernel, ((tiles, rank, LANES), F32), qt, ft)
    p = call(left_kernel, ((tiles, rank, LANES), F32), y, a, p_feedback)

    p = lax.all_to_all(p.reshape(2, tiles // 2 * rank, LANES), "c", 0, 0)
    p = call(pair_kernel, ((tiles // 2 * rank, LANES), F32), p)
    p = lax.all_to_all(p.reshape(replicas, -1, LANES), xy, 0, 0)
    p = share(p, layers, 1.0 / replicas)
    p = lax.all_to_all(p, "z", 0, 0)
    p = share(p, replicas, 1.0)
    p = lax.all_to_all(p, xy, 0, 0).reshape(tiles // 2, rank, LANES)

    rows = columns // 4
    block = pl.BlockSpec((rows, width), lambda i: (i, 0))
    corrected = call(
        corrected_kernel,
        ((columns, width), F32),
        a_full,
        gt,
        ft,
        grid=(columns // rows,),
        in_specs=[
            pl.BlockSpec((tokens, width), lambda i: (0, 0)),
            pl.BlockSpec((rows, tokens), lambda i: (i, 0)),
            block,
        ],
        out_specs=block,
        vmem=57,
        cost_estimate=pl.CostEstimate(
            flops=2 * columns * width * tokens, bytes_accessed=12 * 2**20, transcendentals=0
        ),
    )
    p, corrected = lax.optimization_barrier((p, corrected))

    p_other = lax.ppermute(p, "c", swap)
    q_tiles = -(-columns // LANES)
    place = jnp.stack([lax.axis_index(tensor), lax.axis_index("c")]).astype(jnp.int32)
    p_orth, p_mine, q = call(
        factors_kernel,
        [((tiles, rank, LANES), F32), ((rank, LANES), F32), ((q_tiles, rank, LANES), F32)],
        place,
        p,
        p_other,
        a_full,
        ft,
        gt,
        in_specs=[smem] + [anywhere] * 5,
        out_specs=[anywhere, vmem, vmem],
        scratch_shapes=[
            pltpu.VMEM((tiles, rank, LANES), F32),
            pltpu.VMEM(a_full.shape, BF16),
            pltpu.VMEM(ft.shape, BF16),
            pltpu.VMEM(gt.shape, BF16),
            pltpu.SemaphoreType.DMA((5,)),
        ],
        vmem=57,
    )

    q = lax.all_to_all(q.reshape(replicas, -1, LANES), xy, 0, 0)
    q = share(q, replicas, 1.0 / replicas)
    q = lax.all_to_all(q, xy, 0, 0).reshape(q_tiles, rank, LANES)

    steps = 4
    fbt, q_new = call(
        feedback_out_kernel,
        [((columns, width), BF16), ((rank, columns), F32)],
        q,
        p_orth,
        corrected,
        in_specs=[anywhere] * 3,
        out_specs=[anywhere, vmem],
        scratch_shapes=[
            pltpu.VMEM(q.shape, F32),
            pltpu.VMEM(p_orth.shape, F32),
            pltpu.VMEM(corrected.shape, F32),
            pltpu.VMEM(corrected.shape, BF16),
            pltpu.SemaphoreType.DMA((2,)),
            pltpu.SemaphoreType.DMA((steps,)),
            pltpu.SemaphoreType.DMA((steps,)),
        ],
        vmem=57,
    )
    return fbt.T[None], p_mine.T, q_new.T


def solution(mesh):
    sizes = (4, 8, 8, 2)
    fine = Mesh(mesh.devices.reshape(sizes), ("x", "y", "z", "c"))
    dp, tensor = ("x", "y"), ("z", "c")
    in_specs = (
        P(dp, tensor, None),
        P(dp, None, tensor),
        P(dp, None, tensor),
        P(tensor, None),
    )
    out_specs = (P(dp, None, tensor), P(tensor, None), P(tensor, None))
    return jax.shard_map(body, mesh=fine, in_specs=in_specs, out_specs=out_specs, check_vma=False)
```

```python
import jax
import jax.numpy as jnp
from jax import lax
from jax.experimental import pallas as pl
from jax.experimental.pallas import tpu as pltpu
from jax.sharding import Mesh
from jax.sharding import PartitionSpec as P

LANES = 128
SUBLANES = 8
EPS = 1e-06
KEPT = 1 / 32
BF16 = jnp.bfloat16
F32 = jnp.float32


def split3(value):
    high = value.astype(BF16)
    rest = value - high.astype(F32)
    middle = rest.astype(BF16)
    low = (rest - middle.astype(F32)).astype(BF16)
    return high, middle, low


def stacked(value):
    return jnp.concatenate(split3(value), axis=0)


def unstacked(value):
    rows = value.shape[0] // 3
    return (value[2 * rows :] + value[rows : 2 * rows]) + value[:rows]


def exact_dot(value, exact):
    return unstacked(jnp.dot(stacked(value), exact, preferred_element_type=F32))


def exact_dot_t(value, exact):
    return unstacked(
        lax.dot_general(
            stacked(value), exact, (((1,), (1,)), ((), ())), preferred_element_type=F32
        )
    )


def call(kernel, out_shape, *args, grid=None, vmem=12, **kw):
    shapes = jax.tree.map(lambda s: jax.ShapeDtypeStruct(*s), out_shape, is_leaf=lambda s: isinstance(s, tuple) and isinstance(s[0], tuple))
    return pl.pallas_call(
        kernel,
        out_shape=shapes,
        compiler_params=pltpu.CompilerParams(vmem_limit_bytes=vmem * 2**20),
        **({} if grid is None else {"grid": grid}),
        **kw,
    )(*args)


def started(sources, targets, sems):
    copies = [pltpu.make_async_copy(*pair, sems.at[i]) for i, pair in enumerate(zip(sources, targets))]
    for copy in copies:
        copy.start()
    return copies


def cotangent_kernel(q_hbm, g_hbm, out_ref, q_ref, g_ref, sems):
    for copy in started((q_hbm, g_hbm), (q_ref, g_ref), sems):
        copy.wait()
    rank = q_ref.shape[0]
    half = rank // 2
    product = exact_dot(q_ref[...], g_ref[...])
    low = lax.broadcasted_iota(jnp.int32, (half, LANES), 1) < LANES // 2
    for tile in range(product.shape[1] // LANES):
        block = product[:, tile * LANES : (tile + 1) * LANES]
        top, bottom = block[:half], block[half:]
        out_ref[2 * tile] = jnp.where(low, top, pltpu.roll(bottom, LANES // 2, 1))
        out_ref[2 * tile + 1] = jnp.where(low, pltpu.roll(top, LANES // 2, 1), bottom)


def feedback_kernel(q_ref, f_ref, out_ref):
    product = exact_dot(q_ref[...], f_ref[...])
    for tile in range(out_ref.shape[0]):
        out_ref[tile] = product[:, tile * LANES : (tile + 1) * LANES]


def left_kernel(y_ref, a_ref, pf_ref, out_ref):
    total = y_ref[0]
    for source in range(1, y_ref.shape[0]):
        total = total + y_ref[source]
    tokens = a_ref.shape[0]
    mine = jnp.concatenate([total[:, :tokens], total[:, tokens:]], axis=0)
    product = exact_dot(mine, a_ref[...])
    for tile in range(out_ref.shape[0]):
        out_ref[tile] = product[:, tile * LANES : (tile + 1) * LANES] + pf_ref[tile]


def pair_kernel(x_ref, out_ref):
    out_ref[...] = x_ref[0] + x_ref[1]


def share_kernel(scale, x_ref, out_ref):
    total = x_ref[0]
    for source in range(1, x_ref.shape[0]):
        total = total + x_ref[source]
    total = total * scale
    for target in range(out_ref.shape[0]):
        out_ref[target] = total


def share(x, targets, scale):
    return call(lambda *refs: share_kernel(scale, *refs), ((targets,) + x.shape[1:], F32), x)


def tree_sum(values):
    while len(values) > 1:
        values = [sum(values[i : i + 2]) for i in range(0, len(values), 2)]
    return values[0]


def lane_sum(values):
    return jnp.sum(tree_sum(values), axis=1, keepdims=True)


def sweeps(x_ref):
    tiles, rank, _ = x_ref.shape
    for first in range(0, rank, SUBLANES):

        def sweep(step, carry, first=first):
            position = first + step
            rows = [x_ref[tile, pl.ds(position, 1), :] for tile in range(tiles)]
            dots = lane_sum([x_ref[tile, first:, :] * rows[tile] for tile in range(tiles)])
            square = lane_sum([row * row for row in rows]) + EPS
            order = lax.broadcasted_iota(jnp.int32, dots.shape, 0) + first
            factor = jnp.where(order > position, dots / square, 0.0)
            scale = jnp.where(order == position, 1.0 / jnp.sqrt(square), 1.0)
            for tile in range(tiles):
                x_ref[tile, first:, :] = x_ref[tile, first:, :] * scale - rows[tile] * factor
            return carry

        lax.fori_loop(0, SUBLANES, sweep, 0)


def sweep_group(group):
    index = lax.broadcasted_iota(jnp.int32, (SUBLANES, 1), 0)
    dots = [lane_sum([value * value[i : i + 1, :] for value in group]) for i in range(SUBLANES)]
    least = [dots[i][i : i + 1, :] * KEPT for i in range(SUBLANES)]
    squares = jnp.ones((SUBLANES, 1), F32)
    lost = jnp.zeros((1, 1), F32)
    factors = []
    for i in range(SUBLANES):
        raw = dots[i][i : i + 1, :]
        square = raw + EPS
        lost = jnp.where(raw < least[i], 1.0, lost)
        squares = jnp.where(index == i, square, squares)
        if i + 1 < SUBLANES:
            factor = jnp.where(index > i, dots[i] * (1.0 / square), 0.0)
            factors.append(factor)
            for j in range(i + 1, SUBLANES):
                mine = factor[j : j + 1, :]
                dots[j] = dots[j] - factor * (dots[i][j : j + 1, :] - mine * raw) - mine * dots[i]
    for i, factor in enumerate(factors):
        group = [value - value[i : i + 1, :] * factor for value in group]
    scale = 1.0 / jnp.sqrt(squares)
    return [value * scale for value in group], lost


def orthonormal(x_ref, kept_ref):
    tiles, rank, _ = x_ref.shape
    lost = jnp.zeros((1, 1), F32)
    for first in range(0, rank, SUBLANES):
        group, loss = sweep_group([x_ref[tile, first : first + SUBLANES, :] for tile in range(tiles)])
        lost = jnp.maximum(lost, loss)
        for tile in range(tiles):
            x_ref[tile, first : first + SUBLANES, :] = group[tile]
        if first + SUBLANES == rank:
            break
        overlaps = [lane_sum([value * value[i : i + 1, :] for value in group]) for i in range(SUBLANES - 1)]
        for later in range(first + SUBLANES, rank, SUBLANES):
            values = [x_ref[tile, later : later + SUBLANES, :] for tile in range(tiles)]
            factors = []
            for i in range(SUBLANES):
                row = first + i
                factor = lane_sum([values[tile] * x_ref[tile, row : row + 1, :] for tile in range(tiles)])
                for before in range(i):
                    factor = factor - factors[before] * overlaps[before][i : i + 1, :]
                factors.append(factor)
            for tile in range(tiles):
                change = tree_sum(
                    [x_ref[tile, first + i : first + i + 1, :] * factors[i] for i in range(SUBLANES)]
                )
                x_ref[tile, later : later + SUBLANES, :] = values[tile] - change

    @pl.when(jnp.max(lost) > 0.0)
    def _():
        x_ref[...] = kept_ref[...]
        sweeps(x_ref)


def wide(p_ref):
    return jnp.concatenate([p_ref[tile] for tile in range(p_ref.shape[0])], axis=1)


def pair_dot_t(value, exact):
    rows = value.shape[0]
    high, middle, _ = split3(value)
    product = lax.dot_general(
        jnp.concatenate([high, middle], axis=0),
        exact,
        (((1,), (1,)), ((), ())),
        preferred_element_type=F32,
    )
    return product[rows:] + product[:rows]


def factors_kernel(
    place_ref, mine_ref, other_ref, a_hbm, f_hbm, g_hbm,
    p_ref, p_mine_ref, out_ref,
    kept_ref, a_ref, f_ref, g_ref, sems,
):
    tiles = p_ref.shape[0]
    part = tiles // 2
    member, core = place_ref[0], place_ref[1]
    copies = started((a_hbm, f_hbm, g_hbm), (a_ref, f_ref, g_ref), sems)
    for ref in (p_ref, kept_ref):
        ref[pl.ds(core * part, part)] = mine_ref[...]
        ref[pl.ds((1 - core) * part, part)] = other_ref[...]
    orthonormal(p_ref, kept_ref)
    p_mine_ref[...] = p_ref[member]
    p = wide(p_ref)
    for copy in copies:
        copy.wait()
    product = pair_dot_t(p, f_ref[...])
    product = product + pair_dot_t(pair_dot_t(p, a_ref[...]), g_ref[...])
    width = product.shape[1]
    for tile in range(out_ref.shape[0]):
        block = product[:, tile * LANES : min(width, (tile + 1) * LANES)]
        if block.shape[1] < LANES:
            block = jnp.concatenate([block, jnp.zeros((block.shape[0], LANES - block.shape[1]), F32)], axis=1)
        out_ref[tile] = block


def corrected_kernel(a_ref, g_ref, f_ref, out_ref):
    product = jnp.dot(g_ref[...], a_ref[...], preferred_element_type=F32)
    out_ref[...] = product + f_ref[...].astype(F32)


def feedback_out_kernel(q_ref, p_ref, c_ref, fb_hbm, qt_ref, fb_ref, fb_sems):
    steps = fb_sems.shape[0]
    step = c_ref.shape[1] // steps
    q_wide = wide(q_ref)[:, : qt_ref.shape[1]]
    qt_ref[...] = q_wide
    q1, q2, _ = split3(q_wide.T)
    left = jnp.concatenate([q2, q2, q1, q1], axis=1)
    writes = []
    for i in range(steps):
        at = pl.ds(i * step, step)
        p1, p2, _ = split3(jnp.concatenate([p_ref[t] for t in range(i * step // LANES, (i + 1) * step // LANES)], axis=1))
        right = jnp.concatenate([p2, p1, p2, p1], axis=0)
        low_rank = jnp.dot(left, right, preferred_element_type=F32)
        fb_ref[:, at] = (c_ref[:, at] - low_rank).astype(BF16)
        writes.append(pltpu.make_async_copy(fb_ref.at[:, at], fb_hbm.at[:, at], fb_sems.at[i]))
        writes[-1].start()
    for write in writes:
        write.wait()


def body(activations, out_grad, feedback, q_prev):
    xy, tensor = ("x", "y"), ("z", "c")
    a = activations[0]
    gt = out_grad[0].T
    ft = feedback[0].T
    qt = q_prev.T
    width, columns = ft.shape[1], ft.shape[0]
    rank, tokens = qt.shape[0], gt.shape[1]
    replicas = lax.axis_size(xy)
    members = lax.axis_size(tensor)
    tiles = width // LANES

    swap = [(0, 1), (1, 0)]
    vmem = pl.BlockSpec(memory_space=pltpu.VMEM)
    smem = pl.BlockSpec(memory_space=pltpu.SMEM)
    hbm = pl.BlockSpec(memory_space=pltpu.HBM)

    y = call(
        cotangent_kernel,
        ((members, rank // 2, LANES), F32),
        qt,
        gt,
        in_specs=[hbm, hbm],
        out_specs=vmem,
        scratch_shapes=[pltpu.VMEM(qt.shape, F32), pltpu.VMEM(gt.shape, BF16), pltpu.SemaphoreType.DMA((2,))],
        vmem=57,
    )
    a_late, y = lax.optimization_barrier((a, y))
    a_full = lax.all_gather(a_late, tensor, axis=0, tiled=True)
    y = lax.all_to_all(y, tensor, 0, 0)
    layers = lax.axis_size("z")

    p_feedback = call(feedback_kernel, ((tiles, rank, LANES), F32), qt, ft)
    p = call(left_kernel, ((tiles, rank, LANES), F32), y, a, p_feedback)

    p = lax.all_to_all(p.reshape(2, tiles // 2 * rank, LANES), "c", 0, 0)
    p = call(pair_kernel, ((tiles // 2 * rank, LANES), F32), p)
    p = lax.all_to_all(p.reshape(replicas, -1, LANES), xy, 0, 0)
    p = share(p, layers, 1.0 / replicas)
    p = lax.all_to_all(p, "z", 0, 0)
    p = share(p, replicas, 1.0)
    p = lax.all_to_all(p, xy, 0, 0).reshape(tiles // 2, rank, LANES)

    rows = columns // 4
    block = pl.BlockSpec((rows, width), lambda i: (i, 0))
    corrected = call(
        corrected_kernel,
        ((columns, width), F32),
        a_full,
        gt,
        ft,
        grid=(columns // rows,),
        in_specs=[
            pl.BlockSpec((tokens, width), lambda i: (0, 0)),
            pl.BlockSpec((rows, tokens), lambda i: (i, 0)),
            block,
        ],
        out_specs=block,
        vmem=57,
        cost_estimate=pl.CostEstimate(
            flops=2 * columns * width * tokens, bytes_accessed=12 * 2**20, transcendentals=0
        ),
    )
    p, corrected = lax.optimization_barrier((p, corrected))

    p_other = lax.ppermute(p, "c", swap)
    q_tiles = -(-columns // LANES)
    place = jnp.stack([lax.axis_index(tensor), lax.axis_index("c")]).astype(jnp.int32)
    p_orth, p_mine, q = call(
        factors_kernel,
        [((tiles, rank, LANES), F32), ((rank, LANES), F32), ((q_tiles, rank, LANES), F32)],
        place,
        p,
        p_other,
        a_full,
        ft,
        gt,
        in_specs=[smem, vmem, vmem] + [hbm] * 3,
        out_specs=[vmem] * 3,
        scratch_shapes=[
            pltpu.VMEM((tiles, rank, LANES), F32),
            pltpu.VMEM(a_full.shape, BF16),
            pltpu.VMEM(ft.shape, BF16),
            pltpu.VMEM(gt.shape, BF16),
            pltpu.SemaphoreType.DMA((3,)),
        ],
        vmem=54,
    )

    q = lax.all_to_all(q.reshape(replicas, -1, LANES), xy, 0, 0)
    q = share(q, replicas, 1.0 / replicas)
    q = lax.all_to_all(q, xy, 0, 0).reshape(q_tiles, rank, LANES)

    steps = 4
    fbt, q_new = call(
        feedback_out_kernel,
        [((columns, width), BF16), ((rank, columns), F32)],
        q,
        p_orth,
        corrected,
        in_specs=[vmem] * 3,
        out_specs=[hbm, vmem],
        scratch_shapes=[
            pltpu.VMEM(corrected.shape, BF16),
            pltpu.SemaphoreType.DMA((steps,)),
        ],
        vmem=16,
    )
    return fbt.T[None], p_mine.T, q_new.T


def solution(mesh):
    sizes = (4, 8, 8, 2)
    fine = Mesh(mesh.devices.reshape(sizes), ("x", "y", "z", "c"))
    dp, tensor = ("x", "y"), ("z", "c")
    in_specs = (
        P(dp, tensor, None),
        P(dp, None, tensor),
        P(dp, None, tensor),
        P(tensor, None),
    )
    out_specs = (P(dp, None, tensor), P(tensor, None), P(tensor, None))
    return jax.shard_map(body, mesh=fine, in_specs=in_specs, out_specs=out_specs, check_vma=False)
```

```python
import jax
import jax.numpy as jnp
from jax import lax
from jax.experimental import pallas as pl
from jax.experimental.pallas import tpu as pltpu
from jax.sharding import Mesh
from jax.sharding import PartitionSpec as P

LANES = 128
SUBLANES = 8
EPS = 1e-06
KEPT = 1 / 32
BF16 = jnp.bfloat16
F32 = jnp.float32


def split3(value):
    high = value.astype(BF16)
    rest = value - high.astype(F32)
    middle = rest.astype(BF16)
    low = (rest - middle.astype(F32)).astype(BF16)
    return high, middle, low


def stacked(value):
    return jnp.concatenate(split3(value), axis=0)


def unstacked(value):
    rows = value.shape[0] // 3
    return (value[2 * rows :] + value[rows : 2 * rows]) + value[:rows]


def exact_dot(value, exact):
    return unstacked(jnp.dot(stacked(value), exact, preferred_element_type=F32))


def exact_dot_t(value, exact):
    return unstacked(
        lax.dot_general(
            stacked(value), exact, (((1,), (1,)), ((), ())), preferred_element_type=F32
        )
    )


def call(kernel, out_shape, *args, grid=None, vmem=12, **kw):
    shapes = jax.tree.map(lambda s: jax.ShapeDtypeStruct(*s), out_shape, is_leaf=lambda s: isinstance(s, tuple) and isinstance(s[0], tuple))
    return pl.pallas_call(
        kernel,
        out_shape=shapes,
        compiler_params=pltpu.CompilerParams(vmem_limit_bytes=vmem * 2**20),
        **({} if grid is None else {"grid": grid}),
        **kw,
    )(*args)


def started(sources, targets, sems):
    copies = [pltpu.make_async_copy(*pair, sems.at[i]) for i, pair in enumerate(zip(sources, targets))]
    for copy in copies:
        copy.start()
    return copies


def cotangent_kernel(q_hbm, g_hbm, out_ref, q_ref, g_ref, sems):
    for copy in started((q_hbm, g_hbm), (q_ref, g_ref), sems):
        copy.wait()
    rank = q_ref.shape[0]
    half = rank // 2
    product = exact_dot(q_ref[...], g_ref[...])
    low = lax.broadcasted_iota(jnp.int32, (half, LANES), 1) < LANES // 2
    for tile in range(product.shape[1] // LANES):
        block = product[:, tile * LANES : (tile + 1) * LANES]
        top, bottom = block[:half], block[half:]
        out_ref[2 * tile] = jnp.where(low, top, pltpu.roll(bottom, LANES // 2, 1))
        out_ref[2 * tile + 1] = jnp.where(low, pltpu.roll(top, LANES // 2, 1), bottom)


def feedback_kernel(q_ref, f_ref, out_ref):
    product = exact_dot(q_ref[...], f_ref[...])
    for tile in range(out_ref.shape[0]):
        out_ref[tile] = product[:, tile * LANES : (tile + 1) * LANES]


def left_kernel(y_ref, a_ref, pf_ref, out_ref):
    total = y_ref[0]
    for source in range(1, y_ref.shape[0]):
        total = total + y_ref[source]
    tokens = a_ref.shape[0]
    mine = jnp.concatenate([total[:, :tokens], total[:, tokens:]], axis=0)
    product = exact_dot(mine, a_ref[...])
    for tile in range(out_ref.shape[0]):
        out_ref[tile] = product[:, tile * LANES : (tile + 1) * LANES] + pf_ref[tile]


def pair_kernel(x_ref, out_ref):
    out_ref[...] = x_ref[0] + x_ref[1]


def share_kernel(scale, x_ref, out_ref):
    total = x_ref[0]
    for source in range(1, x_ref.shape[0]):
        total = total + x_ref[source]
    total = total * scale
    for target in range(out_ref.shape[0]):
        out_ref[target] = total


def share(x, targets, scale):
    return call(lambda *refs: share_kernel(scale, *refs), ((targets,) + x.shape[1:], F32), x)


def tree_sum(values):
    while len(values) > 1:
        values = [sum(values[i : i + 2]) for i in range(0, len(values), 2)]
    return values[0]


def lane_sum(values):
    return jnp.sum(tree_sum(values), axis=1, keepdims=True)


def sweeps(x_ref):
    tiles, rank, _ = x_ref.shape
    for first in range(0, rank, SUBLANES):

        def sweep(step, carry, first=first):
            position = first + step
            rows = [x_ref[tile, pl.ds(position, 1), :] for tile in range(tiles)]
            dots = lane_sum([x_ref[tile, first:, :] * rows[tile] for tile in range(tiles)])
            square = lane_sum([row * row for row in rows]) + EPS
            order = lax.broadcasted_iota(jnp.int32, dots.shape, 0) + first
            factor = jnp.where(order > position, dots / square, 0.0)
            scale = jnp.where(order == position, 1.0 / jnp.sqrt(square), 1.0)
            for tile in range(tiles):
                x_ref[tile, first:, :] = x_ref[tile, first:, :] * scale - rows[tile] * factor
            return carry

        lax.fori_loop(0, SUBLANES, sweep, 0)


def sweep_group(group):
    index = lax.broadcasted_iota(jnp.int32, (SUBLANES, 1), 0)
    dots = [lane_sum([value * value[i : i + 1, :] for value in group]) for i in range(SUBLANES)]
    least = [dots[i][i : i + 1, :] * KEPT for i in range(SUBLANES)]
    squares = jnp.ones((SUBLANES, 1), F32)
    lost = jnp.zeros((1, 1), F32)
    factors = []
    for i in range(SUBLANES):
        raw = dots[i][i : i + 1, :]
        square = raw + EPS
        lost = jnp.where(raw < least[i], 1.0, lost)
        squares = jnp.where(index == i, square, squares)
        if i + 1 < SUBLANES:
            factor = jnp.where(index > i, dots[i] * (1.0 / square), 0.0)
            factors.append(factor)
            for j in range(i + 1, SUBLANES):
                mine = factor[j : j + 1, :]
                dots[j] = dots[j] - factor * (dots[i][j : j + 1, :] - mine * raw) - mine * dots[i]
    for i, factor in enumerate(factors):
        group = [value - value[i : i + 1, :] * factor for value in group]
    scale = 1.0 / jnp.sqrt(squares)
    return [value * scale for value in group], lost


def orthonormal(x_ref, kept_ref):
    tiles, rank, _ = x_ref.shape
    lost = jnp.zeros((1, 1), F32)
    for first in range(0, rank, SUBLANES):
        group, loss = sweep_group([x_ref[tile, first : first + SUBLANES, :] for tile in range(tiles)])
        lost = jnp.maximum(lost, loss)
        for tile in range(tiles):
            x_ref[tile, first : first + SUBLANES, :] = group[tile]
        if first + SUBLANES == rank:
            break
        overlaps = [lane_sum([value * value[i : i + 1, :] for value in group]) for i in range(SUBLANES - 1)]
        for later in range(first + SUBLANES, rank, SUBLANES):
            values = [x_ref[tile, later : later + SUBLANES, :] for tile in range(tiles)]
            factors = []
            for i in range(SUBLANES):
                row = first + i
                factor = lane_sum([values[tile] * x_ref[tile, row : row + 1, :] for tile in range(tiles)])
                for before in range(i):
                    factor = factor - factors[before] * overlaps[before][i : i + 1, :]
                factors.append(factor)
            for tile in range(tiles):
                change = tree_sum(
                    [x_ref[tile, first + i : first + i + 1, :] * factors[i] for i in range(SUBLANES)]
                )
                x_ref[tile, later : later + SUBLANES, :] = values[tile] - change

    @pl.when(jnp.max(lost) > 0.0)
    def _():
        x_ref[...] = kept_ref[...]
        sweeps(x_ref)


def wide(p_ref):
    return jnp.concatenate([p_ref[tile] for tile in range(p_ref.shape[0])], axis=1)


def pair_dot_t(value, exact):
    rows = value.shape[0]
    high, middle, _ = split3(value)
    product = lax.dot_general(
        jnp.concatenate([high, middle], axis=0),
        exact,
        (((1,), (1,)), ((), ())),
        preferred_element_type=F32,
    )
    return product[rows:] + product[:rows]


def factors_kernel(
    place_ref, mine_ref, other_ref, high_hbm, middle_hbm,
    p_ref, p_mine_ref, out_ref,
    kept_ref, high_ref, middle_ref, sems,
):
    tiles = p_ref.shape[0]
    part = tiles // 2
    member, core = place_ref[0], place_ref[1]
    copies = started((high_hbm, middle_hbm), (high_ref, middle_ref), sems)
    for ref in (p_ref, kept_ref):
        ref[pl.ds(core * part, part)] = mine_ref[...]
        ref[pl.ds((1 - core) * part, part)] = other_ref[...]
    orthonormal(p_ref, kept_ref)
    p_mine_ref[...] = p_ref[member]
    p = wide(p_ref)
    for copy in copies:
        copy.wait()
    product = pair_dot_t(p, high_ref[...])
    product = product + lax.dot_general(
        p.astype(BF16), middle_ref[...], (((1,), (1,)), ((), ())), preferred_element_type=F32
    )
    width = product.shape[1]
    for tile in range(out_ref.shape[0]):
        block = product[:, tile * LANES : min(width, (tile + 1) * LANES)]
        if block.shape[1] < LANES:
            block = jnp.concatenate([block, jnp.zeros((block.shape[0], LANES - block.shape[1]), F32)], axis=1)
        out_ref[tile] = block


def corrected_kernel(
    a_hbm, g_hbm, f_hbm, out_hbm, high_hbm, middle_hbm,
    a_ref, g_ref, f_ref, out_ref, high_ref, middle_ref, sems, out_sems,
):
    steps = out_sems.shape[1]
    step = out_ref.shape[1] // steps
    for copy in started((g_hbm, a_hbm, f_hbm), (g_ref, a_ref, f_ref), sems):
        copy.wait()
    writes = []
    for i in range(steps):
        at = pl.ds(i * step, step)
        product = jnp.dot(g_ref[...], a_ref[:, at], preferred_element_type=F32)
        corrected = product + f_ref[:, at].astype(F32)
        out_ref[:, at] = corrected
        high_ref[:, at], middle_ref[:, at], _ = split3(corrected)
        refs = ((out_ref, out_hbm), (high_ref, high_hbm), (middle_ref, middle_hbm))
        for j, (source, target) in enumerate(refs):
            writes.append(pltpu.make_async_copy(source.at[:, at], target.at[:, at], out_sems.at[j, i]))
            writes[-1].start()
    for write in writes:
        write.wait()


def feedback_out_kernel(q_ref, p_ref, c_ref, fb_hbm, qt_ref, fb_ref, fb_sems):
    steps = fb_sems.shape[0]
    step = c_ref.shape[1] // steps
    q_wide = wide(q_ref)[:, : qt_ref.shape[1]]
    qt_ref[...] = q_wide
    q1, q2, _ = split3(q_wide.T)
    left = jnp.concatenate([q2, q2, q1, q1], axis=1)
    writes = []
    for i in range(steps):
        at = pl.ds(i * step, step)
        p1, p2, _ = split3(jnp.concatenate([p_ref[t] for t in range(i * step // LANES, (i + 1) * step // LANES)], axis=1))
        right = jnp.concatenate([p2, p1, p2, p1], axis=0)
        low_rank = jnp.dot(left, right, preferred_element_type=F32)
        fb_ref[:, at] = (c_ref[:, at] - low_rank).astype(BF16)
        writes.append(pltpu.make_async_copy(fb_ref.at[:, at], fb_hbm.at[:, at], fb_sems.at[i]))
        writes[-1].start()
    for write in writes:
        write.wait()


def body(activations, out_grad, feedback, q_prev):
    xy, tensor = ("x", "y"), ("z", "c")
    a = activations[0]
    gt = out_grad[0].T
    ft = feedback[0].T
    qt = q_prev.T
    width, columns = ft.shape[1], ft.shape[0]
    rank, tokens = qt.shape[0], gt.shape[1]
    replicas = lax.axis_size(xy)
    members = lax.axis_size(tensor)
    tiles = width // LANES

    swap = [(0, 1), (1, 0)]
    vmem = pl.BlockSpec(memory_space=pltpu.VMEM)
    smem = pl.BlockSpec(memory_space=pltpu.SMEM)
    hbm = pl.BlockSpec(memory_space=pltpu.HBM)

    y = call(
        cotangent_kernel,
        ((members, rank // 2, LANES), F32),
        qt,
        gt,
        in_specs=[hbm, hbm],
        out_specs=vmem,
        scratch_shapes=[pltpu.VMEM(qt.shape, F32), pltpu.VMEM(gt.shape, BF16), pltpu.SemaphoreType.DMA((2,))],
        vmem=57,
    )
    a_late, y = lax.optimization_barrier((a, y))
    a_full = lax.all_gather(a_late, tensor, axis=0, tiled=True)
    y = lax.all_to_all(y, tensor, 0, 0)
    layers = lax.axis_size("z")

    p_feedback = call(feedback_kernel, ((tiles, rank, LANES), F32), qt, ft)
    p = call(left_kernel, ((tiles, rank, LANES), F32), y, a, p_feedback)

    p = lax.all_to_all(p.reshape(2, tiles // 2 * rank, LANES), "c", 0, 0)
    p = call(pair_kernel, ((tiles // 2 * rank, LANES), F32), p)
    p = lax.all_to_all(p.reshape(replicas, -1, LANES), xy, 0, 0)
    p = share(p, layers, 1.0 / replicas)
    p = lax.all_to_all(p, "z", 0, 0)
    p = share(p, replicas, 1.0)
    p = lax.all_to_all(p, xy, 0, 0).reshape(tiles // 2, rank, LANES)

    steps = 4
    corrected, high, middle = call(
        corrected_kernel,
        [((columns, width), F32), ((columns, width), BF16), ((columns, width), BF16)],
        a_full,
        gt,
        ft,
        in_specs=[hbm] * 3,
        out_specs=[hbm] * 3,
        scratch_shapes=[
            pltpu.VMEM(a_full.shape, BF16),
            pltpu.VMEM(gt.shape, BF16),
            pltpu.VMEM(ft.shape, BF16),
            pltpu.VMEM((columns, width), F32),
            pltpu.VMEM((columns, width), BF16),
            pltpu.VMEM((columns, width), BF16),
            pltpu.SemaphoreType.DMA((3,)),
            pltpu.SemaphoreType.DMA((3, steps)),
        ],
        vmem=57,
        cost_estimate=pl.CostEstimate(
            flops=2 * columns * width * tokens, bytes_accessed=12 * 2**20, transcendentals=0
        ),
    )
    p, corrected, high, middle = lax.optimization_barrier((p, corrected, high, middle))

    p_other = lax.ppermute(p, "c", swap)
    q_tiles = -(-columns // LANES)
    place = jnp.stack([lax.axis_index(tensor), lax.axis_index("c")]).astype(jnp.int32)
    p_orth, p_mine, q = call(
        factors_kernel,
        [((tiles, rank, LANES), F32), ((rank, LANES), F32), ((q_tiles, rank, LANES), F32)],
        place,
        p,
        p_other,
        high,
        middle,
        in_specs=[smem, vmem, vmem, hbm, hbm],
        out_specs=[vmem] * 3,
        scratch_shapes=[
            pltpu.VMEM((tiles, rank, LANES), F32),
            pltpu.VMEM(high.shape, BF16),
            pltpu.VMEM(middle.shape, BF16),
            pltpu.SemaphoreType.DMA((2,)),
        ],
        vmem=57,
    )

    q = lax.all_to_all(q.reshape(replicas, -1, LANES), xy, 0, 0)
    q = share(q, replicas, 1.0 / replicas)
    q = lax.all_to_all(q, xy, 0, 0).reshape(q_tiles, rank, LANES)

    steps = 4
    fbt, q_new = call(
        feedback_out_kernel,
        [((columns, width), BF16), ((rank, columns), F32)],
        q,
        p_orth,
        corrected,
        in_specs=[vmem] * 3,
        out_specs=[hbm, vmem],
        scratch_shapes=[
            pltpu.VMEM(corrected.shape, BF16),
            pltpu.SemaphoreType.DMA((steps,)),
        ],
        vmem=16,
    )
    return fbt.T[None], p_mine.T, q_new.T


def solution(mesh):
    sizes = (4, 8, 8, 2)
    fine = Mesh(mesh.devices.reshape(sizes), ("x", "y", "z", "c"))
    dp, tensor = ("x", "y"), ("z", "c")
    in_specs = (
        P(dp, tensor, None),
        P(dp, None, tensor),
        P(dp, None, tensor),
        P(tensor, None),
    )
    out_specs = (P(dp, None, tensor), P(tensor, None), P(tensor, None))
    return jax.shard_map(body, mesh=fine, in_specs=in_specs, out_specs=out_specs, check_vma=False)
```
